32 devices in a mesh: dp: 1, seq: 32 (over z, y, x, core).
Axes of the slice: x: 2, y: 2, z: 4, core: 2. Of those that a mesh axis runs over, the one named last changes fastest.
Arguments:
- tokens: bfloat16 [1, 128, 512, 384], P('dp', 'seq'), may hold values from -6 to 6
- cotangent: bfloat16 [1, 128, 512, 384], P('dp', 'seq'), may hold values from -6 to 6
- wqkv_spatial: bfloat16 [384, 1152], replicated, may hold values from -12.5 to 12.5
- wo_spatial: bfloat16 [384, 384], replicated, may hold values from -0.3125 to 0.3125
- wqkv_temporal: bfloat16 [384, 1152], replicated, may hold values from -12.5 to 12.5
- wo_temporal: bfloat16 [384, 384], replicated, may hold values from -0.3125 to 0.3125
Outputs:
- token_grad: bfloat16 [1, 128, 512, 384], P('dp', 'seq')
- grad_wqkv_spatial: float32 [384, 1152], P(None, 'seq')
- grad_wo_spatial: float32 [384, 384], P(None, 'seq')
- grad_wqkv_temporal: float32 [384, 1152], P(None, 'seq')
- grad_wo_temporal: float32 [384, 384], P(None, 'seq')
The draws below stay inside these ranges and needn't reach their ends.
All inputs are finite; a program needn't handle non-finite values.
Results may differ from the reference program's by a relative error of at most 0.015.
Values may be sent and summed in bfloat16 or wider, within the bound.
A program may use at most 128 MiB of HBM per device.

```python
import jax
import jax.numpy as jnp
from jax import lax

D = 384
HEADS = 6
FRAMES = 128
PATCHES = 512
CLIPS = 1


def projection(key):
    matrix = jnp.clip(jax.random.normal(key, (D, 3 * D), jnp.float32), -4.0, 4.0) * D ** (-0.5)
    return matrix.astype(jnp.bfloat16)


def draw_wqkv_spatial(key, part):
    return projection(jax.random.fold_in(key, 11))


def draw_wqkv_temporal(key, part):
    return projection(jax.random.fold_in(key, 23))


def block_levels(key, extent, cuts, low, largest):
    loudness, own = 1.0, jax.random.fold_in(key, 6)
    for dim, shards_of in cuts:
        draws = jnp.exp(jax.random.uniform(jax.random.fold_in(own, dim), (shards_of,), jnp.float32, low / len(cuts), largest / len(cuts)))
        loudness = loudness * jnp.repeat(draws, extent[dim] // shards_of).reshape([-1 if axis == dim else 1 for axis in range(len(extent))])
    return loudness


def noise(key, extent, scale, limit, shards=(), kind=jnp.bfloat16):
    array = scale * jax.random.normal(key, extent, jnp.float32)
    if shards:
        array = array * block_levels(key, extent, shards, -0.22, 0.18)
    return jnp.clip(array, -limit, limit).astype(kind)


def setup_inputs(seed: int = 0) -> dict:
    arg_keys = jax.random.split(jax.random.key(seed), 7)
    tokens = noise(arg_keys[0], (CLIPS, FRAMES, PATCHES, D), 1.0, 6.0, ((1, 32),))
    cotangent = noise(arg_keys[1], (CLIPS, FRAMES, PATCHES, D), 1.0, 6.0, ((1, 32),))
    wqkv_spatial = draw_wqkv_spatial(jax.random.fold_in(arg_keys[6], 71), 0)
    wo_spatial = noise(arg_keys[3], (D, D), D ** -0.5, 0.3125)
    wqkv_temporal = draw_wqkv_temporal(jax.random.fold_in(arg_keys[6], 71), 0)
    wo_temporal = noise(arg_keys[5], (D, D), D ** -0.5, 0.3125)
    return {"tokens": tokens, "cotangent": cotangent, "wqkv_spatial": wqkv_spatial, "wo_spatial": wo_spatial, "wqkv_temporal": wqkv_temporal, "wo_temporal": wo_temporal}


def product(pattern, left, right):
    return jnp.einsum(pattern, left.astype(jnp.float32), right.astype(jnp.float32))

def normalize(values):
    average = lax.optimization_barrier(jnp.mean(values, -1, keepdims=True))
    centered = values - average
    spread = lax.optimization_barrier(jnp.mean(centered * centered, -1, keepdims=True))
    inverse = lax.rsqrt(spread + 1e-06)
    return (centered * inverse, inverse)

def normalize_back(scaled, inverse, upstream):
    return inverse * (upstream - lax.optimization_barrier(jnp.mean(upstream, -1, keepdims=True)) - scaled * lax.optimization_barrier(jnp.mean(upstream * scaled, -1, keepdims=True)))

def softmax_rounded(queries, key_rows):
    factor = queries.shape[-1] ** (-0.5)
    scores = product('bshe,bthe->bhst', queries, key_rows) * factor
    return jax.nn.softmax(scores, axis=-1).astype(jnp.bfloat16)

def attend(queries, key_rows, values):
    probs = softmax_rounded(queries, key_rows)
    return product('bhst,bthe->bshe', probs, values).astype(jnp.bfloat16)

def attend_back(queries, key_rows, values, upstream):
    factor = queries.shape[-1] ** (-0.5)
    probs = softmax_rounded(queries, key_rows)
    weights = probs.astype(jnp.float32)
    prob_grad = product('bshe,bthe->bhst', upstream, values)
    score_grad = (weights * (prob_grad - lax.optimization_barrier(jnp.sum(weights * prob_grad, -1, keepdims=True))) * factor).astype(jnp.bfloat16)
    query_grad = product('bhst,bthe->bshe', score_grad, key_rows)
    key_grad = product('bhst,bshe->bthe', score_grad, queries)
    value_grad = product('bhst,bshe->bthe', probs, upstream)
    return jnp.concatenate([query_grad, key_grad, value_grad], axis=2)

def grouped(function, arrays, group):
    total_rows = arrays[0].shape[0]
    shaped = tuple((member.reshape((total_rows // group, group) + member.shape[1:]) for member in arrays))
    result = lax.map(lambda bundle: function(*bundle), shaped)
    return result.reshape((total_rows,) + result.shape[2:])

def split_heads(combined):
    shape = combined.shape
    parted = combined.reshape(shape[:-1] + (3, HEADS, shape[-1] // (3 * HEADS)))
    return (parted[..., 0, :, :], parted[..., 1, :, :], parted[..., 2, :, :])

def to_frames(tensor):
    return tensor.reshape((-1,) + tensor.shape[2:])

def to_patches(tensor):
    shape = tensor.shape
    moved = jnp.transpose(tensor, (0, 2, 1, 3, 4))
    return moved.reshape((shape[0] * shape[2], shape[1]) + shape[3:])

def from_patches(tensor, clip_count, patch_count):
    shape = tensor.shape
    joined = tensor.reshape((clip_count, patch_count, shape[1], shape[2] * shape[3]))
    return jnp.transpose(joined, (0, 2, 1, 3))

def reference(tokens, cotangent, wqkv_spatial, wo_spatial, wqkv_temporal, wo_temporal):
    clip_count, frame_count, patch_count, model_width = tokens.shape
    inputs = tokens.astype(jnp.float32)
    scaled_s, inverse_s = normalize(inputs)
    normed_s = scaled_s.astype(jnp.bfloat16)
    combined_s = jnp.dot(normed_s, wqkv_spatial, preferred_element_type=jnp.float32).astype(jnp.bfloat16)
    queries_s, keys_s, values_s = [to_frames(member) for member in split_heads(combined_s)]
    attended_s = grouped(attend, (queries_s, keys_s, values_s), 1).reshape(tokens.shape)
    stream = (inputs + jnp.dot(attended_s, wo_spatial, preferred_element_type=jnp.float32)).astype(jnp.bfloat16)
    scaled_t, inverse_t = normalize(stream.astype(jnp.float32))
    normed_t = scaled_t.astype(jnp.bfloat16)
    combined_t = jnp.dot(normed_t, wqkv_temporal, preferred_element_type=jnp.float32).astype(jnp.bfloat16)
    queries_t, keys_t, values_t = [to_patches(member) for member in split_heads(combined_t)]
    attended_t = from_patches(grouped(attend, (queries_t, keys_t, values_t), 8), clip_count, patch_count)
    grad_wo_t = product('cfpd,cfpe->de', attended_t, cotangent)
    upstream_t = jnp.dot(cotangent, wo_temporal.T, preferred_element_type=jnp.float32).astype(jnp.bfloat16)
    upstream_t = to_patches(upstream_t.reshape(queries_s.shape[:0] + (clip_count, frame_count, patch_count, HEADS, model_width // HEADS)))
    combined_grad_t = from_patches(grouped(attend_back, (queries_t, keys_t, values_t, upstream_t), 8), clip_count, patch_count).astype(jnp.bfloat16)
    grad_wqkv_t = product('cfpd,cfpe->de', normed_t, combined_grad_t)
    input_grad_t = jnp.dot(combined_grad_t, wqkv_temporal.T, preferred_element_type=jnp.float32)
    branch_t = normalize_back(scaled_t, inverse_t, input_grad_t).astype(jnp.bfloat16)
    stream_grad = (cotangent.astype(jnp.float32) + branch_t.astype(jnp.float32)).astype(jnp.bfloat16)
    grad_wo_s = product('cfpd,cfpe->de', attended_s, stream_grad)
    upstream_s = jnp.dot(stream_grad, wo_spatial.T, preferred_element_type=jnp.float32).astype(jnp.bfloat16)
    upstream_s = upstream_s.reshape(queries_s.shape)
    combined_grad_s = grouped(attend_back, (queries_s, keys_s, values_s, upstream_s), 1)
    combined_grad_s = combined_grad_s.reshape(combined_s.shape).astype(jnp.bfloat16)
    grad_wqkv_s = product('cfpd,cfpe->de', normed_s, combined_grad_s)
    input_grad_s = jnp.dot(combined_grad_s, wqkv_spatial.T, preferred_element_type=jnp.float32)
    token_grad = (stream_grad.astype(jnp.float32) + normalize_back(scaled_s, inverse_s, input_grad_s)).astype(jnp.bfloat16)
    factor = (clip_count * frame_count * patch_count) ** (-0.5)
    return (token_grad, grad_wqkv_s * factor, grad_wo_s * factor, grad_wqkv_t * factor, grad_wo_t * factor)
```

```python
import functools
import math

import jax
import jax.numpy as jnp
from jax import lax
from jax.experimental import pallas as pl
from jax.experimental.pallas import tpu as pltpu
from jax.sharding import PartitionSpec as P

HEADS = 6
PAIR = 128
MESH = pl.DeviceIdType.MESH
BF16 = jnp.bfloat16
F32 = jnp.float32
VMEM_LIMIT = 56 * 1024 * 1024


def nn(left, right):
    return lax.dot_general(left, right, (((1,), (0,)), ((), ())), preferred_element_type=F32)


def nt(left, right):
    return lax.dot_general(left, right, (((1,), (1,)), ((), ())), preferred_element_type=F32)


def tn(left, right):
    return lax.dot_general(left, right, (((0,), (0,)), ((), ())), preferred_element_type=F32)


def normalize(values):
    average = jnp.mean(values, -1, keepdims=True)
    centered = values - average
    spread = jnp.mean(centered * centered, -1, keepdims=True)
    inverse = lax.rsqrt(spread + 1e-06)
    return (centered * inverse, inverse)


def normalize_back(scaled, inverse, upstream):
    return inverse * (
        upstream
        - jnp.mean(upstream, -1, keepdims=True)
        - scaled * jnp.mean(upstream * scaled, -1, keepdims=True)
    )


def two_heads(rows):
    first = lax.broadcasted_iota(jnp.int32, rows.shape, 1) < PAIR // 2
    none = jnp.zeros_like(rows)
    return jnp.concatenate([jnp.where(first, rows, none), jnp.where(first, none, rows)], 0)


def own_head(both):
    group = both.shape[1] // 2
    first = lax.broadcasted_iota(jnp.int32, (PAIR, group), 0) < PAIR // 2
    return jnp.where(first, both[:, :group], both[:, group:]).T


def pair_forward(queries, keys, values):
    scores = nt(keys, two_heads(queries))
    factor = math.log2(math.e) * (PAIR // 2) ** (-0.5)
    powers = jnp.exp2((scores - jnp.max(scores, 0, keepdims=True)) * factor)
    probs = (powers * (1.0 / jnp.sum(powers, 0, keepdims=True))).astype(BF16)
    return probs, own_head(tn(values, probs)).astype(BF16)


def pair_backward(queries, keys, values, upstream, probs):
    upstream = two_heads(upstream)
    prob_grad = nt(values, upstream)
    weights = probs.astype(F32)
    total = jnp.sum(weights * prob_grad, 0, keepdims=True)
    factor = (PAIR // 2) ** (-0.5)
    score_grad = (weights * ((prob_grad - total) * factor)).astype(BF16)
    query_grad = own_head(tn(keys, score_grad)).astype(BF16)
    key_grad = nn(score_grad, two_heads(queries)).astype(BF16)
    value_grad = nn(probs, upstream).astype(BF16)
    return query_grad, key_grad, value_grad


def three(combined, pair, width):
    return [combined[..., k * width + pair * PAIR : k * width + (pair + 1) * PAIR] for k in range(3)]


def offset(step, n):
    return (step % 2) * (n // 2) + step // 2


def greet(me, n):
    barrier = pltpu.get_barrier_semaphore()

    def say(step, carry):
        pl.semaphore_signal(
            barrier, inc=1, device_id={"seq": lax.rem(me + step, n)}, device_id_type=MESH
        )
        return carry

    lax.fori_loop(1, n, say, 0)
    pl.semaphore_wait(barrier, n - 1)


def each_other(n, body):
    def run(step, carry):
        body(offset(step, n))
        return carry

    lax.fori_loop(1, n, run, 0)


def forward_kernel(
    n, x_ref, wqkv_ref, wo_ref, cot_ref,
    probs_ref, combined_ref, attended_ref, stream_out, cot_out,
    rows, send, recv, cot_send, cot_recv, local,
):
    frame = pl.program_id(0)
    frames = pl.num_programs(0)
    me = lax.axis_index("seq")
    width = x_ref.shape[-1]

    def cot_copy(k):
        to = lax.rem(me + k, n)
        return pltpu.make_async_remote_copy(
            src_ref=cot_ref.at[:, to], dst_ref=cot_out.at[me],
            send_sem=cot_send.at[k], recv_sem=cot_recv.at[k],
            device_id={"seq": to}, device_id_type=MESH,
        )

    def frame_copy(k):
        to = lax.rem(me + k, n)
        return pltpu.make_async_remote_copy(
            src_ref=rows.at[frame, to], dst_ref=stream_out.at[me, frame],
            send_sem=send.at[k], recv_sem=recv.at[k],
            device_id={"seq": to}, device_id_type=MESH,
        )

    def stream_copy(k):
        to = lax.rem(me + k, n)
        return pltpu.make_async_remote_copy(
            src_ref=rows.at[:, to], dst_ref=stream_out.at[me],
            send_sem=send.at[k], recv_sem=recv.at[k],
            device_id={"seq": to}, device_id_type=MESH,
        )

    own_cot = pltpu.make_async_copy(cot_ref.at[:, me], cot_out.at[me], local.at[0])
    own_stream = pltpu.make_async_copy(rows.at[:, me], stream_out.at[me], local.at[1])

    @pl.when(frame == 0)
    def _():
        greet(me, n)
        each_other(n, lambda k: cot_copy(k).start())
        own_cot.start()

    x = x_ref[0].astype(F32)
    scaled, _ = normalize(x)
    combined = nn(scaled.astype(BF16), wqkv_ref[...]).astype(BF16)
    combined_ref[0] = combined
    heads = []
    for pair in range(width // PAIR):
        probs, out = pair_forward(*three(combined, pair, width))
        probs_ref[0, pair] = probs
        heads.append(out)
    attended = jnp.concatenate(heads, 1)
    attended_ref[0] = attended
    stream = (x + nn(attended, wo_ref[...])).astype(BF16)
    rows[frame] = stream.reshape(rows.shape[1:])
    each_other(n, lambda k: frame_copy(k).start())

    @pl.when(frame == frames - 1)
    def _():
        own_stream.start()
        own_cot.wait()
        own_stream.wait()

        def finish(k):
            cot_copy(k).wait()
            stream_copy(k).wait()

        each_other(n, finish)


def temporal_kernel(
    n, stream_ref, cot_ref, wqkv_ref, wo_ref,
    wqkv_grad_ref, wo_grad_ref, branch_out,
    stream_rows, cot_rows, rows, wqkv_sum, wo_sum, send, recv, local,
):
    me = lax.axis_index("seq")
    local_frames, patches, width = branch_out.shape[0], branch_out.shape[2], branch_out.shape[3]
    frames = n * local_frames
    together = min(4, patches)
    greet(me, n)
    lanes = width // PAIR
    for c in range(lanes):
        stream_rows[c] = stream_ref[:, c * PAIR : (c + 1) * PAIR].astype(F32)
        cot_rows[c] = cot_ref[:, c * PAIR : (c + 1) * PAIR].astype(F32)
    wqkv_sum[...] = jnp.zeros_like(wqkv_sum)
    wo_sum[...] = jnp.zeros_like(wo_sum)

    def group(number, carry):
        first = number * together
        spots = [pl.ds(first + i, frames, stride=patches) for i in range(together)]

        def gather(ref):
            return jnp.concatenate(
                [jnp.concatenate([ref[c, s, :] for s in spots], 0) for c in range(lanes)], 1
            )

        scaled, inverse = normalize(gather(stream_rows))
        normed = scaled.astype(BF16)
        cot = gather(cot_rows).astype(BF16)
        combined = nn(normed, wqkv_ref[...]).astype(BF16)
        upstream = nt(cot, wo_ref[...]).astype(BF16)
        outs, grads = [], []
        for i in range(together):
            part = slice(i * frames, (i + 1) * frames)
            out, grad = [], []
            for pair in range(width // PAIR):
                q, k, v = three(combined[part], pair, width)
                probs, attended = pair_forward(q, k, v)
                up = upstream[part, pair * PAIR : (pair + 1) * PAIR]
                out.append(attended)
                grad.append(pair_backward(q, k, v, up, probs))
            outs.append(jnp.concatenate(out, 1))
            grads.append(jnp.concatenate([g[j] for j in range(3) for g in grad], 1))
        attended = jnp.concatenate(outs, 0)
        combined_grad = jnp.concatenate(grads, 0)
        wo_sum[...] += tn(cot, attended)
        wqkv_sum[...] += tn(combined_grad, normed)
        branch = normalize_back(scaled, inverse, nt(combined_grad, wqkv_ref[...]))
        for i, s in enumerate(spots):
            for c in range(lanes):
                stream_rows[c, s, :] = branch[
                    i * frames : (i + 1) * frames, c * PAIR : (c + 1) * PAIR
                ]
        return carry

    lax.fori_loop(0, patches // together, group, 0)
    for c in range(lanes):
        part = stream_rows[c].astype(BF16)
        rows[:, :, :, c * PAIR : (c + 1) * PAIR] = part.reshape(rows.shape[:3] + (PAIR,))

    def copy(k):
        to = lax.rem(me + k, n)
        return pltpu.make_async_remote_copy(
            src_ref=rows.at[to], dst_ref=branch_out.at[:, me],
            send_sem=send.at[k], recv_sem=recv.at[k],
            device_id={"seq": to}, device_id_type=MESH,
        )

    each_other(n, lambda k: copy(k).start())
    own = pltpu.make_async_copy(rows.at[me], branch_out.at[:, me], local.at[0])
    own.start()
    scale = (lax.axis_size("dp") * frames * patches * n) ** (-0.5)
    wqkv_grad_ref[...] = (wqkv_sum[...] * scale).astype(BF16)
    wo_grad_ref[...] = (wo_sum[...] * scale).astype(BF16)
    own.wait()
    each_other(n, lambda k: copy(k).wait())


def backward_kernel(
    scale, x_ref, cot_ref, branch_ref, probs_ref, combined_ref, attended_ref, wqkv_ref, wo_ref,
    token_grad_ref, wqkv_grad_ref, wo_grad_ref, wqkv_sum, wo_sum,
):
    frame = pl.program_id(0)
    width = x_ref.shape[-1]

    @pl.when(frame == 0)
    def _():
        wqkv_sum[...] = jnp.zeros_like(wqkv_sum)
        wo_sum[...] = jnp.zeros_like(wo_sum)

    stream_grad = (cot_ref[0].astype(F32) + branch_ref[0].astype(F32)).astype(BF16)
    wo_sum[...] += tn(stream_grad, attended_ref[0])
    upstream = nt(stream_grad, wo_ref[...]).astype(BF16)
    combined = combined_ref[0]
    grads = []
    for pair in range(width // PAIR):
        q, k, v = three(combined, pair, width)
        up = upstream[:, pair * PAIR : (pair + 1) * PAIR]
        grads.append(pair_backward(q, k, v, up, probs_ref[0, pair]))
    combined_grad = jnp.concatenate([g[j] for j in range(3) for g in grads], 1)
    scaled, inverse = normalize(x_ref[0].astype(F32))
    wqkv_sum[...] += tn(combined_grad, scaled.astype(BF16))
    input_grad = nt(combined_grad, wqkv_ref[...])
    token_grad_ref[0] = (
        stream_grad.astype(F32) + normalize_back(scaled, inverse, input_grad)
    ).astype(BF16)

    @pl.when(frame == pl.num_programs(0) - 1)
    def _():
        wqkv_grad_ref[...] = (wqkv_sum[...] * scale).astype(BF16)
        wo_grad_ref[...] = (wo_sum[...] * scale).astype(BF16)


def scatter_sum(wqkv_grad, wo_grad, n):
    width = wqkv_grad.shape[1]
    mine = jnp.concatenate(
        [wqkv_grad.reshape(n, -1, width), wo_grad.reshape(n, -1, width)], 1
    )
    me = lax.axis_index("seq")
    bit = 1
    while bit < n:
        side = lax.rem(me // bit, 2)
        halves = mine.reshape((mine.shape[0] // 2, 2) + mine.shape[1:])
        keep = lax.dynamic_index_in_dim(halves, side, 1, keepdims=False)
        give = lax.dynamic_index_in_dim(halves, 1 - side, 1, keepdims=False).astype(BF16)
        pairs = [(i, i ^ bit) for i in range(n)]
        got = lax.ppermute(give, "seq", pairs)
        mine = keep.astype(F32) + got.astype(F32)
        bit *= 2
    mine = lax.psum(mine[0], "dp")
    split = wqkv_grad.shape[0] // n
    return mine[:split].T, mine[split:].T


def full(shape):
    return pl.BlockSpec(shape, lambda f: (0,) * len(shape))


def per_frame(shape):
    return pl.BlockSpec((1,) + shape, lambda f: (f,) + (0,) * len(shape))


def on_device(tokens, cotangent, wqkv_spatial, wo_spatial, wqkv_temporal, wo_temporal):
    clips, frames, count, width = tokens.shape
    n = lax.axis_size("seq")
    patches = count // n
    total = frames * clips
    pairs = width // PAIR
    x = tokens.reshape(total, count, width)
    cot = cotangent.reshape(total, count, width)
    anywhere = pl.BlockSpec(memory_space=pl.ANY)
    whole = pl.BlockSpec(memory_space=pltpu.VMEM)
    shape = jax.ShapeDtypeStruct
    dma = pltpu.SemaphoreType.DMA
    probs, combined, attended, stream_t, cot_t = pl.pallas_call(
        functools.partial(forward_kernel, n),
        grid=(total,),
        in_specs=[
            per_frame((count, width)), full(wqkv_spatial.shape), full(wo_spatial.shape), anywhere,
        ],
        out_specs=[
            per_frame((pairs, count, 2 * count)), per_frame((count, 3 * width)),
            per_frame((count, width)), anywhere, anywhere,
        ],
        out_shape=[
            shape((total, pairs, count, 2 * count), BF16),
            shape((total, count, 3 * width), BF16),
            shape((total, count, width), BF16),
            shape((n, total, patches, width), BF16),
            shape((n, total, patches, width), BF16),
        ],
        scratch_shapes=[
            pltpu.VMEM((total, n, patches, width), BF16),
            dma((n,)), dma((n,)), dma((n,)), dma((n,)), dma((2,)),
        ],
        compiler_params=pltpu.CompilerParams(
            collective_id=0, has_side_effects=True, vmem_limit_bytes=VMEM_LIMIT
        ),
        name="spatial_forward",
    )(x, wqkv_spatial, wo_spatial, cot.reshape(total, n, patches, width))

    tokens_t = n * total * patches
    wqkv_grad_t, wo_grad_t, branch = pl.pallas_call(
        functools.partial(temporal_kernel, n),
        in_specs=[whole] * 4,
        out_specs=[whole, whole, anywhere],
        out_shape=[
            shape((3 * width, width), BF16),
            shape((width, width), BF16),
            shape((total, n, patches, width), BF16),
        ],
        scratch_shapes=[
            pltpu.VMEM((width // PAIR, tokens_t, PAIR), F32),
            pltpu.VMEM((width // PAIR, tokens_t, PAIR), F32),
            pltpu.VMEM((n, total, patches, width), BF16),
            pltpu.VMEM((3 * width, width), F32),
            pltpu.VMEM((width, width), F32),
            dma((n,)), dma((n,)), dma((1,)),
        ],
        compiler_params=pltpu.CompilerParams(
            collective_id=1, has_side_effects=True, vmem_limit_bytes=VMEM_LIMIT
        ),
        name="temporal",
    )(
        stream_t.reshape(tokens_t, width), cot_t.reshape(tokens_t, width),
        wqkv_temporal, wo_temporal,
    )

    scale = (total * count * n * lax.axis_size("dp")) ** (-0.5)
    token_grad, wqkv_grad_s, wo_grad_s = pl.pallas_call(
        functools.partial(backward_kernel, scale),
        grid=(total,),
        in_specs=[
            per_frame((count, width)), per_frame((count, width)), per_frame((count, width)),
            per_frame((pairs, count, 2 * count)), per_frame((count, 3 * width)),
            per_frame((count, width)), full(wqkv_spatial.shape), full(wo_spatial.shape),
        ],
        out_specs=[
            per_frame((count, width)), full((3 * width, width)), full((width, width)),
        ],
        out_shape=[
            shape((total, count, width), BF16),
            shape((3 * width, width), BF16),
            shape((width, width), BF16),
        ],
        scratch_shapes=[pltpu.VMEM((3 * width, width), F32), pltpu.VMEM((width, width), F32)],
        compiler_params=pltpu.CompilerParams(vmem_limit_bytes=VMEM_LIMIT),
        cost_estimate=pl.CostEstimate(
            flops=20 * total * count * width * (width + count),
            bytes_accessed=2 * total * count * (pairs * 2 * count + 8 * width),
            transcendentals=0,
        ),
        name="spatial_backward",
    )(
        x, cot, branch.reshape(total, count, width), probs, combined, attended,
        wqkv_spatial, wo_spatial,
    )
    wqkv_t, wo_t = scatter_sum(wqkv_grad_t, wo_grad_t, n)
    wqkv_s, wo_s = scatter_sum(wqkv_grad_s, wo_grad_s, n)
    return (token_grad.reshape(tokens.shape), wqkv_s, wo_s, wqkv_t, wo_t)


def solution(mesh):
    in_specs = (P("dp", "seq", None, None), P("dp", "seq", None, None), P(), P(), P(), P())
    out_specs = (
        P("dp", "seq", None, None),
        P(None, "seq"),
        P(None, "seq"),
        P(None, "seq"),
        P(None, "seq"),
    )
    return jax.shard_map(
        on_device, mesh=mesh, in_specs=in_specs, out_specs=out_specs, check_vma=False
    )
```

```python
import functools
import math

import jax
import jax.numpy as jnp
from jax import lax
from jax.experimental import pallas as pl
from jax.experimental.pallas import tpu as pltpu
from jax.sharding import PartitionSpec as P

HEADS = 6
PAIR = 128
MESH = pl.DeviceIdType.MESH
BF16 = jnp.bfloat16
F32 = jnp.float32
VMEM_LIMIT = 60 * 1024 * 1024


def nn(left, right):
    return lax.dot_general(left, right, (((1,), (0,)), ((), ())), preferred_element_type=F32)


def nt(left, right):
    return lax.dot_general(left, right, (((1,), (1,)), ((), ())), preferred_element_type=F32)


def tn(left, right):
    return lax.dot_general(left, right, (((0,), (0,)), ((), ())), preferred_element_type=F32)


def normalize(values):
    average = jnp.mean(values, -1, keepdims=True)
    centered = values - average
    spread = jnp.mean(centered * centered, -1, keepdims=True)
    inverse = lax.rsqrt(spread + 1e-06)
    return (centered * inverse, inverse)


def normalize_back(scaled, inverse, upstream):
    return inverse * (
        upstream
        - jnp.mean(upstream, -1, keepdims=True)
        - scaled * jnp.mean(upstream * scaled, -1, keepdims=True)
    )


def two_heads(rows):
    first = lax.broadcasted_iota(jnp.int32, rows.shape, 1) < PAIR // 2
    none = jnp.zeros_like(rows)
    return jnp.concatenate([jnp.where(first, rows, none), jnp.where(first, none, rows)], 0)


def own_head(both):
    group = both.shape[1] // 2
    first = lax.broadcasted_iota(jnp.int32, (PAIR, group), 0) < PAIR // 2
    return jnp.where(first, both[:, :group], both[:, group:]).T


def pair_forward(queries, keys, values):
    scores = nt(keys, two_heads(queries))
    factor = math.log2(math.e) * (PAIR // 2) ** (-0.5)
    powers = jnp.exp2((scores - jnp.max(scores, 0, keepdims=True)) * factor)
    probs = (powers * (1.0 / jnp.sum(powers, 0, keepdims=True))).astype(BF16)
    return probs, own_head(tn(values, probs)).astype(BF16)


def pair_backward(queries, keys, values, upstream, probs):
    upstream = two_heads(upstream)
    prob_grad = nt(values, upstream)
    weights = probs.astype(F32)
    total = jnp.sum(weights * prob_grad, 0, keepdims=True)
    factor = (PAIR // 2) ** (-0.5)
    score_grad = (weights * ((prob_grad - total) * factor)).astype(BF16)
    query_grad = own_head(tn(keys, score_grad)).astype(BF16)
    key_grad = nn(score_grad, two_heads(queries)).astype(BF16)
    value_grad = nn(probs, upstream).astype(BF16)
    return query_grad, key_grad, value_grad


def three(combined, pair, width):
    return [combined[..., k * width + pair * PAIR : k * width + (pair + 1) * PAIR] for k in range(3)]


def offset(step, n):
    return (step % 2) * (n // 2) + step // 2


def greet(me, n):
    barrier = pltpu.get_barrier_semaphore()

    def say(step, carry):
        pl.semaphore_signal(
            barrier, inc=1, device_id={"seq": lax.rem(me + step, n)}, device_id_type=MESH
        )
        return carry

    lax.fori_loop(1, n, say, 0)
    pl.semaphore_wait(barrier, n - 1)


def each_other(n, body):
    def run(step, carry):
        body(offset(step, n))
        return carry

    lax.fori_loop(1, n, run, 0)


def kernel(
    n, halves, x_ref, cot_ref, wqkv_s_ref, wo_s_ref, wqkv_t_ref, wo_t_ref,
    token_grad_ref, wqkv_grad_s_ref, wo_grad_s_ref, wqkv_grad_t_ref, wo_grad_t_ref,
    probs_s, combined_s, attended_s, cot_send, stream_send, branch_send,
    cot_recv, stream_recv, branch_recv, stream_rows, cot_rows, wqkv_sum, wo_sum,
    cot_sems, stream_sems, branch_sems,
):
    me = lax.axis_index("seq")
    frames, count, width = x_ref.shape
    lanes = width // PAIR
    span = cot_send.shape[2] // frames
    together = 2 if halves == 2 else 1
    steps = frames // together
    slab = together * span
    all_frames = n * frames
    scale = (lax.axis_size("dp") * all_frames * count) ** (-0.5)

    def slab_of(step):
        return slice(None) if steps == 1 else pl.ds(pl.multiple_of(step * slab, slab), slab)

    def put(ref, step, members):
        parts = [member.reshape(n, halves, span, width) for member in members]
        for half in range(halves):
            rows = [part[:, half] for part in parts]
            ref[half, :, slab_of(step), :] = jnp.concatenate(rows, 1).astype(BF16)

    def get(ref, step):
        parts = [ref[half, :, slab_of(step), :].astype(F32) for half in range(halves)]
        return [
            jnp.concatenate([part[:, i * span : (i + 1) * span] for part in parts], 1).reshape(
                count, width
            )
            for i in range(together)
        ]

    def half_copy(source, target, sems, half, k):
        to = lax.rem(me + k, n)
        return pltpu.make_async_remote_copy(
            src_ref=source.at[half, to], dst_ref=target.at[half, me],
            send_sem=sems.at[0, half, k], recv_sem=sems.at[1, half, k],
            device_id={"seq": to}, device_id_type=MESH,
        )

    def slab_copy(half, step, k):
        to = lax.rem(me + k, n)
        return pltpu.make_async_remote_copy(
            src_ref=branch_send.at[half, to, slab_of(step)],
            dst_ref=branch_recv.at[half, me, slab_of(step)],
            send_sem=branch_sems.at[0, half, step, k], recv_sem=branch_sems.at[1, half, step, k],
            device_id={"seq": to}, device_id_type=MESH,
        )

    def cot_copy(half, k):
        return half_copy(cot_send, cot_recv, cot_sems, half, k)

    def stream_copy(half, k):
        return half_copy(stream_send, stream_recv, stream_sems, half, k)

    for step in range(steps):
        members = range(step * together, (step + 1) * together)
        put(cot_send, step, [cot_ref[frame].astype(F32) for frame in members])
    greet(me, n)
    each_other(n, lambda k: cot_copy(0, k).start())

    def forward(step, carry):
        streams = []
        for i in range(together):
            frame = step * together + i
            x = x_ref[frame].astype(F32)
            scaled, _ = normalize(x)
            combined = nn(scaled.astype(BF16), wqkv_s_ref[...]).astype(BF16)
            combined_s[frame] = combined
            heads = []
            for pair in range(lanes):
                probs, out = pair_forward(*three(combined, pair, width))
                probs_s[frame, pair] = probs
                heads.append(out)
            attended = jnp.concatenate(heads, 1)
            attended_s[frame] = attended
            streams.append(x + nn(attended, wo_s_ref[...]))
        put(stream_send, step, streams)
        return carry

    lax.fori_loop(0, steps, forward, 0)
    each_other(n, lambda k: stream_copy(0, k).start())
    for half in range(1, halves):
        each_other(n, lambda k: cot_copy(half, k).start())
        each_other(n, lambda k: stream_copy(half, k).start())
    for half in range(halves):
        cot_recv[half, me] = cot_send[half, me]
        stream_recv[half, me] = stream_send[half, me]

    wqkv_sum[...] = jnp.zeros_like(wqkv_sum)
    wo_sum[...] = jnp.zeros_like(wo_sum)
    few = min(4, span)

    def temporal(number, carry):
        spots = [pl.ds(number * few + i, all_frames, stride=span) for i in range(few)]

        def gather(ref):
            return jnp.concatenate(
                [jnp.concatenate([ref[c, s, :] for s in spots], 0) for c in range(lanes)], 1
            )

        scaled, inverse = normalize(gather(stream_rows))
        normed = scaled.astype(BF16)
        cot = gather(cot_rows).astype(BF16)
        combined = nn(normed, wqkv_t_ref[...]).astype(BF16)
        upstream = nt(cot, wo_t_ref[...]).astype(BF16)
        outs, grads = [], []
        for i in range(few):
            part = slice(i * all_frames, (i + 1) * all_frames)
            out, grad = [], []
            for pair in range(lanes):
                q, k, v = three(combined[part], pair, width)
                probs, attended = pair_forward(q, k, v)
                up = upstream[part, pair * PAIR : (pair + 1) * PAIR]
                out.append(attended)
                grad.append(pair_backward(q, k, v, up, probs))
            outs.append(jnp.concatenate(out, 1))
            grads.append(jnp.concatenate([g[j] for j in range(3) for g in grad], 1))
        attended = jnp.concatenate(outs, 0)
        combined_grad = jnp.concatenate(grads, 0)
        wo_sum[...] += tn(cot, attended)
        wqkv_sum[...] += tn(combined_grad, normed)
        branch = normalize_back(scaled, inverse, nt(combined_grad, wqkv_t_ref[...]))
        for i, s in enumerate(spots):
            for c in range(lanes):
                stream_rows[c, s, :] = branch[
                    i * all_frames : (i + 1) * all_frames, c * PAIR : (c + 1) * PAIR
                ]
        return carry

    for half in range(halves):

        def arrive(k):
            cot_copy(half, k).wait_recv()
            stream_copy(half, k).wait_recv()

        each_other(n, arrive)
        for c in range(lanes):
            part = slice(c * PAIR, (c + 1) * PAIR)
            flat = stream_rows.shape[1:]
            stream_rows[c] = stream_recv[half, :, :, part].astype(F32).reshape(flat)
            cot_rows[c] = cot_recv[half, :, :, part].astype(F32).reshape(flat)
        lax.fori_loop(0, span // few, temporal, 0)
        for c in range(lanes):
            part = stream_rows[c].reshape(branch_send.shape[1:3] + (PAIR,)).astype(BF16)
            branch_send[half, :, :, c * PAIR : (c + 1) * PAIR] = part
        for step in range(steps):
            each_other(n, lambda k: slab_copy(half, step, k).start())
        branch_recv[half, me] = branch_send[half, me]

    wqkv_grad_t_ref[...] = (wqkv_sum[...] * scale).astype(BF16)
    wo_grad_t_ref[...] = (wo_sum[...] * scale).astype(BF16)
    wqkv_sum[...] = jnp.zeros_like(wqkv_sum)
    wo_sum[...] = jnp.zeros_like(wo_sum)

    def backward(step, carry):
        def arrive(k):
            for half in range(halves):
                slab_copy(half, step, k).wait_recv()

        each_other(n, arrive)
        for i, branch in enumerate(get(branch_recv, step)):
            frame = step * together + i
            stream_grad = (cot_ref[frame].astype(F32) + branch).astype(BF16)
            wo_sum[...] += tn(stream_grad, attended_s[frame])
            upstream = nt(stream_grad, wo_s_ref[...]).astype(BF16)
            combined = combined_s[frame]
            grads = []
            for pair in range(lanes):
                q, k, v = three(combined, pair, width)
                up = upstream[:, pair * PAIR : (pair + 1) * PAIR]
                grads.append(pair_backward(q, k, v, up, probs_s[frame, pair]))
            combined_grad = jnp.concatenate([g[j] for j in range(3) for g in grads], 1)
            scaled, inverse = normalize(x_ref[frame].astype(F32))
            wqkv_sum[...] += tn(combined_grad, scaled.astype(BF16))
            input_grad = nt(combined_grad, wqkv_s_ref[...])
            token_grad_ref[frame] = (
                stream_grad.astype(F32) + normalize_back(scaled, inverse, input_grad)
            ).astype(BF16)
        return carry

    lax.fori_loop(0, steps, backward, 0)
    wqkv_grad_s_ref[...] = (wqkv_sum[...] * scale).astype(BF16)
    wo_grad_s_ref[...] = (wo_sum[...] * scale).astype(BF16)

    def left(k):
        for half in range(halves):
            cot_copy(half, k).wait_send()
            stream_copy(half, k).wait_send()
            for step in range(steps):
                slab_copy(half, step, k).wait_send()

    each_other(n, left)


def scatter_sum(wqkv_grad, wo_grad, n):
    width = wqkv_grad.shape[1]
    mine = jnp.concatenate(
        [wqkv_grad.reshape(n, -1, width), wo_grad.reshape(n, -1, width)], 1
    )
    me = lax.axis_index("seq")
    bit = 1
    while bit < n:
        side = lax.rem(me // bit, 2)
        halves = mine.reshape((mine.shape[0] // 2, 2) + mine.shape[1:])
        keep = lax.dynamic_index_in_dim(halves, side, 1, keepdims=False)
        give = lax.dynamic_index_in_dim(halves, 1 - side, 1, keepdims=False).astype(BF16)
        pairs = [(i, i ^ bit) for i in range(n)]
        got = lax.ppermute(give, "seq", pairs)
        mine = keep.astype(F32) + got.astype(F32)
        bit *= 2
    mine = lax.psum(mine[0], "dp")
    split = wqkv_grad.shape[0] // n
    return mine[:split].T, mine[split:].T


def on_device(tokens, cotangent, wqkv_spatial, wo_spatial, wqkv_temporal, wo_temporal):
    clips, frames, count, width = tokens.shape
    n = lax.axis_size("seq")
    patches = count // n
    total = frames * clips
    pairs = width // PAIR
    halves = 2 if patches == 16 and total % 2 == 0 else 1
    span = patches // halves
    whole = pl.BlockSpec(memory_space=pltpu.VMEM)
    shape = jax.ShapeDtypeStruct
    sems = pltpu.SemaphoreType.DMA
    exchanged = pltpu.VMEM((halves, n, total * span, width), BF16)
    gathered = pltpu.VMEM((pairs, n * total * span, PAIR), F32)
    token_grad, wqkv_grad_s, wo_grad_s, wqkv_grad_t, wo_grad_t = pl.pallas_call(
        functools.partial(kernel, n, halves),
        in_specs=[whole] * 6,
        out_specs=[whole] * 5,
        out_shape=[shape((total, count, width), BF16)]
        + [shape((3 * width, width), BF16), shape((width, width), BF16)] * 2,
        scratch_shapes=[
            pltpu.VMEM((total, pairs, count, 2 * count), BF16),
            pltpu.VMEM((total, count, 3 * width), BF16),
            pltpu.VMEM((total, count, width), BF16),
        ]
        + [exchanged] * 6
        + [gathered] * 2
        + [
            pltpu.VMEM((3 * width, width), F32),
            pltpu.VMEM((width, width), F32),
            sems((2, halves, n)), sems((2, halves, n)),
            sems((2, halves, max(total // 2, 1), n)),
        ],
        compiler_params=pltpu.CompilerParams(
            collective_id=0, has_side_effects=True, vmem_limit_bytes=VMEM_LIMIT
        ),
        name="space_time_backward",
    )(
        tokens.reshape(total, count, width), cotangent.reshape(total, count, width),
        wqkv_spatial, wo_spatial, wqkv_temporal, wo_temporal,
    )
    wqkv_t, wo_t = scatter_sum(wqkv_grad_t, wo_grad_t, n)
    wqkv_s, wo_s = scatter_sum(wqkv_grad_s, wo_grad_s, n)
    return (token_grad.reshape(tokens.shape), wqkv_s, wo_s, wqkv_t, wo_t)


def solution(mesh):
    in_specs = (P("dp", "seq", None, None), P("dp", "seq", None, None), P(), P(), P(), P())
    out_specs = (
        P("dp", "seq", None, None),
        P(None, "seq"),
        P(None, "seq"),
        P(None, "seq"),
        P(None, "seq"),
    )
    return jax.shard_map(
        on_device, mesh=mesh, in_specs=in_specs, out_specs=out_specs, check_vma=False
    )
```

```python
import functools
import math

import jax
import jax.numpy as jnp
import numpy as np
from jax import lax
from jax.experimental import pallas as pl
from jax.experimental.pallas import tpu as pltpu
from jax.sharding import PartitionSpec as P

HEADS = 6
PAIR = 128
MESH = pl.DeviceIdType.MESH
BF16 = jnp.bfloat16
F32 = jnp.float32
VMEM_LIMIT = 60 * 1024 * 1024


def nn(left, right):
    return lax.dot_general(left, right, (((1,), (0,)), ((), ())), preferred_element_type=F32)


def nt(left, right):
    return lax.dot_general(left, right, (((1,), (1,)), ((), ())), preferred_element_type=F32)


def tn(left, right):
    return lax.dot_general(left, right, (((0,), (0,)), ((), ())), preferred_element_type=F32)


def normalize(values):
    average = jnp.mean(values, -1, keepdims=True)
    centered = values - average
    spread = jnp.mean(centered * centered, -1, keepdims=True)
    inverse = lax.rsqrt(spread + 1e-06)
    return (centered * inverse, inverse)


def normalize_back(scaled, inverse, upstream):
    return inverse * (
        upstream
        - jnp.mean(upstream, -1, keepdims=True)
        - scaled * jnp.mean(upstream * scaled, -1, keepdims=True)
    )


def two_heads(rows):
    first = lax.broadcasted_iota(jnp.int32, rows.shape, 1) < PAIR // 2
    none = jnp.zeros_like(rows)
    return jnp.concatenate([jnp.where(first, rows, none), jnp.where(first, none, rows)], 0)


def own_head(both):
    group = both.shape[1] // 2
    first = lax.broadcasted_iota(jnp.int32, (PAIR, group), 0) < PAIR // 2
    return jnp.where(first, both[:, :group], both[:, group:]).T


def pair_forward(queries, keys, values):
    scores = nt(keys, two_heads(queries))
    factor = math.log2(math.e) * (PAIR // 2) ** (-0.5)
    powers = jnp.exp2((scores - jnp.max(scores, 0, keepdims=True)) * factor)
    probs = (powers * (1.0 / jnp.sum(powers, 0, keepdims=True))).astype(BF16)
    return probs, own_head(tn(values, probs)).astype(BF16)


def pair_backward(queries, keys, values, upstream, probs):
    upstream = two_heads(upstream)
    prob_grad = nt(values, upstream)
    weights = probs.astype(F32)
    total = jnp.sum(weights * prob_grad, 0, keepdims=True)
    factor = (PAIR // 2) ** (-0.5)
    score_grad = (weights * ((prob_grad - total) * factor)).astype(BF16)
    query_grad = own_head(tn(keys, score_grad)).astype(BF16)
    key_grad = nn(score_grad, two_heads(queries)).astype(BF16)
    value_grad = nn(probs, upstream).astype(BF16)
    return query_grad, key_grad, value_grad


def three(combined, pair, width):
    return [combined[..., k * width + pair * PAIR : k * width + (pair + 1) * PAIR] for k in range(3)]


def offset(step, n):
    return (step % 2) * (n // 2) + step // 2


def greet(me, n):
    barrier = pltpu.get_barrier_semaphore()

    def say(step, carry):
        pl.semaphore_signal(
            barrier, inc=1, device_id={"seq": lax.rem(me + step, n)}, device_id_type=MESH
        )
        return carry

    lax.fori_loop(1, n, say, 0)
    pl.semaphore_wait(barrier, n - 1)


def each_other(n, body):
    def run(step, carry):
        body(offset(step, n))
        return carry

    lax.fori_loop(1, n, run, 0)


def kernel(
    n, halves, inside, x_ref, cot_ref, wqkv_s_ref, wo_s_ref, wqkv_t_ref, wo_t_ref, places_ref,
    token_grad_ref, grads_ref,
    probs_s, combined_s, attended_s, cot_send, stream_send, branch_send,
    cot_recv, stream_recv, branch_recv, stream_rows, cot_rows, wqkv_sum, wo_sum,
    cot_sems, stream_sems, branch_sems, mine, grads, give, got, sum_sems,
):
    me = lax.axis_index("seq")
    frames, count, width = x_ref.shape
    lanes = width // PAIR
    span = cot_send.shape[2] // frames
    together = 2 if halves == 2 else 1
    steps = frames // together
    slab = together * span
    all_frames = n * frames
    scale = (lax.axis_size("dp") * all_frames * count) ** (-0.5)

    def slab_of(step):
        return slice(None) if steps == 1 else pl.ds(pl.multiple_of(step * slab, slab), slab)

    def put(ref, step, members):
        parts = [member.reshape(n, halves, span, width) for member in members]
        for half in range(halves):
            rows = [part[:, half] for part in parts]
            ref[half, :, slab_of(step), :] = jnp.concatenate(rows, 1).astype(BF16)

    def get(ref, step):
        parts = [ref[half, :, slab_of(step), :].astype(F32) for half in range(halves)]
        return [
            jnp.concatenate([part[:, i * span : (i + 1) * span] for part in parts], 1).reshape(
                count, width
            )
            for i in range(together)
        ]

    def half_copy(source, target, sems, half, k):
        to = lax.rem(me + k, n)
        return pltpu.make_async_remote_copy(
            src_ref=source.at[half, to], dst_ref=target.at[half, me],
            send_sem=sems.at[0, half, k], recv_sem=sems.at[1, half, k],
            device_id={"seq": to}, device_id_type=MESH,
        )

    def slab_copy(half, step, k):
        to = lax.rem(me + k, n)
        return pltpu.make_async_remote_copy(
            src_ref=branch_send.at[half, to, slab_of(step)],
            dst_ref=branch_recv.at[half, me, slab_of(step)],
            send_sem=branch_sems.at[0, half, step, k], recv_sem=branch_sems.at[1, half, step, k],
            device_id={"seq": to}, device_id_type=MESH,
        )

    def cot_copy(half, k):
        return half_copy(cot_send, cot_recv, cot_sems, half, k)

    def stream_copy(half, k):
        return half_copy(stream_send, stream_recv, stream_sems, half, k)

    bits = n.bit_length() - 1
    most = 2 * width
    piece = 256

    def sum_copy(which, level):
        bit, rows = 1 << level, most >> level
        side = lax.rem(me // bit, 2)
        spot = pl.ds(2 * most - 2 * rows, rows)
        copy = pltpu.make_async_remote_copy(
            src_ref=give.at[which, spot], dst_ref=got.at[which, spot],
            send_sem=sum_sems.at[0, which, level], recv_sem=sum_sems.at[1, which, level],
            device_id={"seq": me + bit * (1 - 2 * side)}, device_id_type=MESH,
        )
        return copy, side, rows, spot

    def placed(start):
        lane = lax.broadcasted_iota(jnp.int32, (piece, 4 * width), 1)
        here = places_ref[pl.ds(pl.multiple_of(start, piece), piece), :] == lane
        return nn(jnp.where(here, 1.0, 0.0).astype(BF16), grads[...])

    def sum_start(which, level):
        copy, side, rows, spot = sum_copy(which, level)
        if level == 0:

            def fill(number, carry):
                at = pl.ds(pl.multiple_of(number * piece, piece), piece)
                give[which, at, :] = placed((1 - side) * most + number * piece).astype(BF16)
                return carry

            lax.fori_loop(0, most // piece, fill, 0)
            copy.start()

            def keep(number, carry):
                at = pl.ds(pl.multiple_of(number * piece, piece), piece)
                mine[at, :] = placed(side * most + number * piece)
                return carry

            lax.fori_loop(0, most // piece, keep, 0)
        else:
            other = pl.ds(pl.multiple_of((1 - side) * rows, 16), rows)
            give[which, spot, :] = mine[other, :].astype(BF16)
            copy.start()

    def sum_finish(which, level):
        copy, side, rows, spot = sum_copy(which, level)
        copy.wait()
        own = pl.ds(0, rows) if level == 0 else pl.ds(pl.multiple_of(side * rows, 16), rows)
        mine[0:rows, :] = mine[own, :] + got[which, spot, :].astype(F32)
        if level == bits - 1:
            grads_ref[which] = mine[0:rows, :]

    def close(which):
        target = grads if inside else grads_ref.at[which]
        target[0 : 3 * width, :] = (wqkv_sum[...] * scale).astype(BF16)
        target[3 * width :, :] = (wo_sum[...] * scale).astype(BF16)
        wqkv_sum[...] = jnp.zeros_like(wqkv_sum)
        wo_sum[...] = jnp.zeros_like(wo_sum)
        if inside:
            sum_start(which, 0)

    def advance(which, level):
        sum_finish(which, level)
        if level + 1 < bits:
            sum_start(which, level + 1)

    for step in range(steps):
        members = range(step * together, (step + 1) * together)
        put(cot_send, step, [cot_ref[frame].astype(F32) for frame in members])
    greet(me, n)
    each_other(n, lambda k: cot_copy(0, k).start())

    def forward(step, carry):
        streams = []
        for i in range(together):
            frame = step * together + i
            x = x_ref[frame].astype(F32)
            scaled, _ = normalize(x)
            combined = nn(scaled.astype(BF16), wqkv_s_ref[...]).astype(BF16)
            combined_s[frame] = combined
            heads = []
            for pair in range(lanes):
                probs, out = pair_forward(*three(combined, pair, width))
                probs_s[frame, pair] = probs
                heads.append(out)
            attended = jnp.concatenate(heads, 1)
            attended_s[frame] = attended
            streams.append(x + nn(attended, wo_s_ref[...]))
        put(stream_send, step, streams)
        return carry

    lax.fori_loop(0, steps, forward, 0)
    each_other(n, lambda k: stream_copy(0, k).start())
    for half in range(1, halves):
        each_other(n, lambda k: cot_copy(half, k).start())
        each_other(n, lambda k: stream_copy(half, k).start())
    for half in range(halves):
        cot_recv[half, me] = cot_send[half, me]
        stream_recv[half, me] = stream_send[half, me]

    wqkv_sum[...] = jnp.zeros_like(wqkv_sum)
    wo_sum[...] = jnp.zeros_like(wo_sum)
    few = min(4, span)

    def temporal(number, carry):
        spots = [pl.ds(number * few + i, all_frames, stride=span) for i in range(few)]

        def gather(ref):
            return jnp.concatenate(
                [jnp.concatenate([ref[c, s, :] for s in spots], 0) for c in range(lanes)], 1
            )

        scaled, inverse = normalize(gather(stream_rows))
        normed = scaled.astype(BF16)
        cot = gather(cot_rows).astype(BF16)
        combined = nn(normed, wqkv_t_ref[...]).astype(BF16)
        upstream = nt(cot, wo_t_ref[...]).astype(BF16)
        outs, grads = [], []
        for i in range(few):
            part = slice(i * all_frames, (i + 1) * all_frames)
            out, grad = [], []
            for pair in range(lanes):
                q, k, v = three(combined[part], pair, width)
                probs, attended = pair_forward(q, k, v)
                up = upstream[part, pair * PAIR : (pair + 1) * PAIR]
                out.append(attended)
                grad.append(pair_backward(q, k, v, up, probs))
            outs.append(jnp.concatenate(out, 1))
            grads.append(jnp.concatenate([g[j] for j in range(3) for g in grad], 1))
        attended = jnp.concatenate(outs, 0)
        combined_grad = jnp.concatenate(grads, 0)
        wo_sum[...] += tn(cot, attended)
        wqkv_sum[...] += tn(combined_grad, normed)
        branch = normalize_back(scaled, inverse, nt(combined_grad, wqkv_t_ref[...]))
        for i, s in enumerate(spots):
            for c in range(lanes):
                stream_rows[c, s, :] = branch[
                    i * all_frames : (i + 1) * all_frames, c * PAIR : (c + 1) * PAIR
                ]
        return carry

    for half in range(halves):

        def arrive(k):
            cot_copy(half, k).wait_recv()
            stream_copy(half, k).wait_recv()

        each_other(n, arrive)
        for c in range(lanes):
            part = slice(c * PAIR, (c + 1) * PAIR)
            flat = stream_rows.shape[1:]
            stream_rows[c] = stream_recv[half, :, :, part].astype(F32).reshape(flat)
            cot_rows[c] = cot_recv[half, :, :, part].astype(F32).reshape(flat)
        lax.fori_loop(0, span // few, temporal, 0)
        for c in range(lanes):
            part = stream_rows[c].reshape(branch_send.shape[1:3] + (PAIR,)).astype(BF16)
            branch_send[half, :, :, c * PAIR : (c + 1) * PAIR] = part
        for step in range(steps):
            each_other(n, lambda k: slab_copy(half, step, k).start())
        branch_recv[half, me] = branch_send[half, me]

    close(0)

    def backward(step, carry):
        def arrive(k):
            for half in range(halves):
                slab_copy(half, step, k).wait_recv()

        each_other(n, arrive)
        for i, branch in enumerate(get(branch_recv, step)):
            frame = step * together + i
            for level in range(bits if inside else 0):
                pl.when(frame == level)(functools.partial(advance, 0, level))
            stream_grad = (cot_ref[frame].astype(F32) + branch).astype(BF16)
            wo_sum[...] += tn(stream_grad, attended_s[frame])
            upstream = nt(stream_grad, wo_s_ref[...]).astype(BF16)
            combined = combined_s[frame]
            grads = []
            for pair in range(lanes):
                q, k, v = three(combined, pair, width)
                up = upstream[:, pair * PAIR : (pair + 1) * PAIR]
                grads.append(pair_backward(q, k, v, up, probs_s[frame, pair]))
            combined_grad = jnp.concatenate([g[j] for j in range(3) for g in grads], 1)
            scaled, inverse = normalize(x_ref[frame].astype(F32))
            wqkv_sum[...] += tn(combined_grad, scaled.astype(BF16))
            input_grad = nt(combined_grad, wqkv_s_ref[...])
            token_grad_ref[frame] = (
                stream_grad.astype(F32) + normalize_back(scaled, inverse, input_grad)
            ).astype(BF16)
        return carry

    lax.fori_loop(0, steps, backward, 0)
    if inside:
        for level in range(frames, bits):
            advance(0, level)
    close(1)
    if inside:
        for level in range(bits):
            advance(1, level)

    def left(k):
        for half in range(halves):
            cot_copy(half, k).wait_send()
            stream_copy(half, k).wait_send()
            for step in range(steps):
                slab_copy(half, step, k).wait_send()

    each_other(n, left)


def scatter_sum(wqkv_grad, wo_grad, n):
    width = wqkv_grad.shape[1]
    mine = jnp.concatenate(
        [wqkv_grad.reshape(n, -1, width), wo_grad.reshape(n, -1, width)], 1
    )
    me = lax.axis_index("seq")
    bit = 1
    while bit < n:
        side = lax.rem(me // bit, 2)
        halves = mine.reshape((mine.shape[0] // 2, 2) + mine.shape[1:])
        keep = lax.dynamic_index_in_dim(halves, side, 1, keepdims=False)
        give = lax.dynamic_index_in_dim(halves, 1 - side, 1, keepdims=False).astype(BF16)
        pairs = [(i, i ^ bit) for i in range(n)]
        got = lax.ppermute(give, "seq", pairs)
        mine = keep.astype(F32) + got.astype(F32)
        bit *= 2
    mine = lax.psum(mine[0], "dp")
    split = wqkv_grad.shape[0] // n
    return mine[:split].T, mine[split:].T


def on_device(tokens, cotangent, wqkv_spatial, wo_spatial, wqkv_temporal, wo_temporal):
    clips, frames, count, width = tokens.shape
    n = lax.axis_size("seq")
    patches = count // n
    total = frames * clips
    pairs = width // PAIR
    halves = 2 if patches == 16 and total % 2 == 0 else 1
    span = patches // halves
    bits = n.bit_length() - 1
    split = width // n
    inside = n == 1 << bits and 4 * split % 16 == 0 and bits > 0
    owners = [int(format(i, "b").zfill(bits)[::-1], 2) for i in range(n if inside else 0)]
    places = np.zeros((8, 1), np.int32)
    if inside:
        own = [
            [3 * split * j + i for i in range(3 * split)]
            + [3 * width + split * j + i for i in range(split)]
            for j in owners
        ]
        places = np.array(own, np.int32).reshape(-1, 1)
    whole = pl.BlockSpec(memory_space=pltpu.VMEM)
    shape = jax.ShapeDtypeStruct
    sems = pltpu.SemaphoreType.DMA
    exchanged = pltpu.VMEM((halves, n, total * span, width), BF16)
    gathered = pltpu.VMEM((pairs, n * total * span, PAIR), F32)
    sums = shape((2, 4 * split, width), F32) if inside else shape((2, 4 * width, width), BF16)
    token_grad, grads = pl.pallas_call(
        functools.partial(kernel, n, halves, inside),
        in_specs=[whole] * 7,
        out_specs=[whole] * 2,
        out_shape=[shape((total, count, width), BF16), sums],
        scratch_shapes=[
            pltpu.VMEM((total, pairs, count, 2 * count), BF16),
            pltpu.VMEM((total, count, 3 * width), BF16),
            pltpu.VMEM((total, count, width), BF16),
        ]
        + [exchanged] * 6
        + [gathered] * 2
        + [
            pltpu.VMEM((3 * width, width), F32),
            pltpu.VMEM((width, width), F32),
            sems((2, halves, n)), sems((2, halves, n)),
            sems((2, halves, max(total // 2, 1), n)),
            pltpu.VMEM((2 * width if inside else 8, width), F32),
            pltpu.VMEM((4 * width if inside else 16, width), BF16),
            pltpu.VMEM((2, 4 * width if inside else 16, width), BF16),
            pltpu.VMEM((2, 4 * width if inside else 16, width), BF16),
            sems((2, 2, max(bits, 1))),
        ],
        compiler_params=pltpu.CompilerParams(
            collective_id=0, has_side_effects=True, vmem_limit_bytes=VMEM_LIMIT
        ),
        name="space_time_backward",
    )(
        tokens.reshape(total, count, width), cotangent.reshape(total, count, width),
        wqkv_spatial, wo_spatial, wqkv_temporal, wo_temporal, jnp.asarray(places),
    )
    if inside:
        grads = lax.psum(grads, "dp")
        wqkv_t, wqkv_s = [part[: 3 * split].T for part in grads]
        wo_t, wo_s = [part[3 * split :].T for part in grads]
    else:
        wqkv_t, wo_t = scatter_sum(grads[0, : 3 * width], grads[0, 3 * width :], n)
        wqkv_s, wo_s = scatter_sum(grads[1, : 3 * width], grads[1, 3 * width :], n)
    return (token_grad.reshape(tokens.shape), wqkv_s, wo_s, wqkv_t, wo_t)


def solution(mesh):
    in_specs = (P("dp", "seq", None, None), P("dp", "seq", None, None), P(), P(), P(), P())
    out_specs = (
        P("dp", "seq", None, None),
        P(None, "seq"),
        P(None, "seq"),
        P(None, "seq"),
        P(None, "seq"),
    )
    return jax.shard_map(
        on_device, mesh=mesh, in_specs=in_specs, out_specs=out_specs, check_vma=False
    )
```

```python
import functools
import math

import jax
import jax.numpy as jnp
import numpy as np
from jax import lax
from jax.experimental import pallas as pl
from jax.experimental.pallas import tpu as pltpu
from jax.sharding import PartitionSpec as P

HEADS = 6
PAIR = 128
MESH = pl.DeviceIdType.MESH
BF16 = jnp.bfloat16
F32 = jnp.float32
VMEM_LIMIT = 60 * 1024 * 1024


def nn(left, right):
    return lax.dot_general(left, right, (((1,), (0,)), ((), ())), preferred_element_type=F32)


def nt(left, right):
    return lax.dot_general(left, right, (((1,), (1,)), ((), ())), preferred_element_type=F32)


def tn(left, right):
    return lax.dot_general(left, right, (((0,), (0,)), ((), ())), preferred_element_type=F32)


def normalize(values):
    average = jnp.mean(values, -1, keepdims=True)
    centered = values - average
    spread = jnp.mean(centered * centered, -1, keepdims=True)
    inverse = lax.rsqrt(spread + 1e-06)
    return (centered * inverse, inverse)


def normalize_back(scaled, inverse, upstream):
    return inverse * (
        upstream
        - jnp.mean(upstream, -1, keepdims=True)
        - scaled * jnp.mean(upstream * scaled, -1, keepdims=True)
    )


def two_heads(rows):
    first = lax.broadcasted_iota(jnp.int32, rows.shape, 1) < PAIR // 2
    none = jnp.zeros_like(rows)
    return jnp.concatenate([jnp.where(first, rows, none), jnp.where(first, none, rows)], 0)


def own_head(both):
    group = both.shape[1] // 2
    first = lax.broadcasted_iota(jnp.int32, (PAIR, group), 0) < PAIR // 2
    return jnp.where(first, both[:, :group], both[:, group:]).T


def pair_forward(queries, keys, values):
    scores = nt(keys, two_heads(queries))
    factor = math.log2(math.e) * (PAIR // 2) ** (-0.5)
    powers = jnp.exp2((scores - jnp.max(scores, 0, keepdims=True)) * factor)
    probs = (powers * (1.0 / jnp.sum(powers, 0, keepdims=True))).astype(BF16)
    return probs, own_head(tn(values, probs)).astype(BF16)


def pair_backward(queries, keys, values, upstream, probs):
    upstream = two_heads(upstream)
    prob_grad = nt(values, upstream)
    weights = probs.astype(F32)
    total = jnp.sum(weights * prob_grad, 0, keepdims=True)
    factor = (PAIR // 2) ** (-0.5)
    score_grad = (weights * ((prob_grad - total) * factor)).astype(BF16)
    query_grad = own_head(tn(keys, score_grad)).astype(BF16)
    key_grad = nn(score_grad, two_heads(queries)).astype(BF16)
    value_grad = nn(probs, upstream).astype(BF16)
    return query_grad, key_grad, value_grad


def three(combined, pair, width):
    return [combined[..., k * width + pair * PAIR : k * width + (pair + 1) * PAIR] for k in range(3)]


def offset(step, n):
    return (step % 2) * (n // 2) + step // 2


def greet(me, n):
    barrier = pltpu.get_barrier_semaphore()

    def say(step, carry):
        pl.semaphore_signal(
            barrier, inc=1, device_id={"seq": lax.rem(me + step, n)}, device_id_type=MESH
        )
        return carry

    lax.fori_loop(1, n, say, 0)
    pl.semaphore_wait(barrier, n - 1)


def each_other(n, body):
    def run(step, carry):
        body(offset(step, n))
        return carry

    lax.fori_loop(1, n, run, 0)


def kernel(
    n, halves, inside, x_ref, cot_ref, wqkv_s_ref, wo_s_ref, wqkv_t_ref, wo_t_ref, places_ref,
    token_grad_ref, grads_ref,
    probs_s, combined_s, attended_s, cot_send, stream_send, branch_send,
    cot_recv, stream_recv, branch_recv, stream_rows, cot_rows, wqkv_sum, wo_sum,
    cot_sems, stream_sems, branch_sems, mine, grads, give, got, sum_sems,
):
    me = lax.axis_index("seq")
    frames, count, width = x_ref.shape
    lanes = width // PAIR
    span = cot_send.shape[2] // frames
    together = 2 if halves == 2 else 1
    steps = frames // together
    slab = together * span
    all_frames = n * frames
    scale = (lax.axis_size("dp") * all_frames * count) ** (-0.5)

    def slab_of(step):
        return slice(None) if steps == 1 else pl.ds(pl.multiple_of(step * slab, slab), slab)

    def put(ref, step, members):
        parts = [member.reshape(n, halves, span, width) for member in members]
        for half in range(halves):
            rows = [part[:, half] for part in parts]
            ref[half, :, slab_of(step), :] = jnp.concatenate(rows, 1).astype(BF16)

    def get(ref, step):
        parts = [ref[half, :, slab_of(step), :].astype(F32) for half in range(halves)]
        return [
            jnp.concatenate([part[:, i * span : (i + 1) * span] for part in parts], 1).reshape(
                count, width
            )
            for i in range(together)
        ]

    def half_copy(source, target, sems, half, k):
        to = lax.rem(me + k, n)
        return pltpu.make_async_remote_copy(
            src_ref=source.at[half, to], dst_ref=target.at[half, me],
            send_sem=sems.at[0, half, k], recv_sem=sems.at[1, half, k],
            device_id={"seq": to}, device_id_type=MESH,
        )

    def slab_copy(half, step, k):
        to = lax.rem(me + k, n)
        return pltpu.make_async_remote_copy(
            src_ref=branch_send.at[half, to, slab_of(step)],
            dst_ref=branch_recv.at[half, me, slab_of(step)],
            send_sem=branch_sems.at[0, half, step, k], recv_sem=branch_sems.at[1, half, step, k],
            device_id={"seq": to}, device_id_type=MESH,
        )

    def cot_copy(half, k):
        return half_copy(cot_send, cot_recv, cot_sems, half, k)

    def stream_copy(half, k):
        return half_copy(stream_send, stream_recv, stream_sems, half, k)

    bits = n.bit_length() - 1
    most = 2 * width
    piece = 256

    def sum_copy(which, level):
        bit, rows = 1 << level, most >> level
        side = lax.rem(me // bit, 2)
        spot = pl.ds(2 * most - 2 * rows, rows)
        copy = pltpu.make_async_remote_copy(
            src_ref=give.at[which, spot], dst_ref=got.at[which, spot],
            send_sem=sum_sems.at[0, which, level], recv_sem=sum_sems.at[1, which, level],
            device_id={"seq": me + bit * (1 - 2 * side)}, device_id_type=MESH,
        )
        return copy, side, rows, spot

    def placed(start):
        lane = lax.broadcasted_iota(jnp.int32, (piece, 4 * width), 1)
        here = places_ref[pl.ds(pl.multiple_of(start, piece), piece), :] == lane
        return nn(jnp.where(here, 1.0, 0.0).astype(BF16), grads[...])

    def sum_start(which, level):
        copy, side, rows, spot = sum_copy(which, level)
        if level == 0:

            def fill(number, carry):
                at = pl.ds(pl.multiple_of(number * piece, piece), piece)
                give[which, at, :] = placed((1 - side) * most + number * piece).astype(BF16)
                return carry

            lax.fori_loop(0, most // piece, fill, 0)
            copy.start()

            def keep(number, carry):
                at = pl.ds(pl.multiple_of(number * piece, piece), piece)
                mine[which, at, :] = placed(side * most + number * piece)
                return carry

            lax.fori_loop(0, most // piece, keep, 0)
        else:
            other = pl.ds(pl.multiple_of((1 - side) * rows, 16), rows)
            give[which, spot, :] = mine[which, other, :].astype(BF16)
            copy.start()

    def sum_finish(which, level):
        copy, side, rows, spot = sum_copy(which, level)
        copy.wait()
        own = pl.ds(0, rows) if level == 0 else pl.ds(pl.multiple_of(side * rows, 16), rows)
        mine[which, 0:rows, :] = mine[which, own, :] + got[which, spot, :].astype(F32)
        if level == bits - 1:
            grads_ref[which] = mine[which, 0:rows, :]

    def close(which):
        target = grads if inside else grads_ref.at[which]
        target[0 : 3 * width, :] = (wqkv_sum[...] * scale).astype(BF16)
        target[3 * width :, :] = (wo_sum[...] * scale).astype(BF16)
        wqkv_sum[...] = jnp.zeros_like(wqkv_sum)
        wo_sum[...] = jnp.zeros_like(wo_sum)
        if inside:
            sum_start(which, 0)

    def advance(which, level):
        sum_finish(which, level)
        if level + 1 < bits:
            sum_start(which, level + 1)

    for step in range(steps):
        members = range(step * together, (step + 1) * together)
        put(cot_send, step, [cot_ref[frame].astype(F32) for frame in members])
    greet(me, n)
    each_other(n, lambda k: cot_copy(0, k).start())

    def forward(step, carry):
        streams = []
        for i in range(together):
            frame = step * together + i
            x = x_ref[frame].astype(F32)
            scaled, _ = normalize(x)
            combined = nn(scaled.astype(BF16), wqkv_s_ref[...]).astype(BF16)
            combined_s[frame] = combined
            heads = []
            for pair in range(lanes):
                probs, out = pair_forward(*three(combined, pair, width))
                probs_s[frame, pair] = probs
                heads.append(out)
            attended = jnp.concatenate(heads, 1)
            attended_s[frame] = attended
            streams.append(x + nn(attended, wo_s_ref[...]))
        put(stream_send, step, streams)
        return carry

    lax.fori_loop(0, steps, forward, 0)
    each_other(n, lambda k: stream_copy(0, k).start())
    for half in range(1, halves):
        each_other(n, lambda k: cot_copy(half, k).start())
        each_other(n, lambda k: stream_copy(half, k).start())
    for half in range(halves):
        cot_recv[half, me] = cot_send[half, me]
        stream_recv[half, me] = stream_send[half, me]

    wqkv_sum[...] = jnp.zeros_like(wqkv_sum)
    wo_sum[...] = jnp.zeros_like(wo_sum)
    few = min(4, span)

    def temporal(number, carry):
        spots = [pl.ds(number * few + i, all_frames, stride=span) for i in range(few)]

        def gather(ref):
            return jnp.concatenate(
                [jnp.concatenate([ref[c, s, :] for s in spots], 0) for c in range(lanes)], 1
            )

        scaled, inverse = normalize(gather(stream_rows))
        normed = scaled.astype(BF16)
        cot = gather(cot_rows).astype(BF16)
        combined = nn(normed, wqkv_t_ref[...]).astype(BF16)
        upstream = nt(cot, wo_t_ref[...]).astype(BF16)
        outs, grads = [], []
        for i in range(few):
            part = slice(i * all_frames, (i + 1) * all_frames)
            out, grad = [], []
            for pair in range(lanes):
                q, k, v = three(combined[part], pair, width)
                probs, attended = pair_forward(q, k, v)
                up = upstream[part, pair * PAIR : (pair + 1) * PAIR]
                out.append(attended)
                grad.append(pair_backward(q, k, v, up, probs))
            outs.append(jnp.concatenate(out, 1))
            grads.append(jnp.concatenate([g[j] for j in range(3) for g in grad], 1))
        attended = jnp.concatenate(outs, 0)
        combined_grad = jnp.concatenate(grads, 0)
        wo_sum[...] += tn(cot, attended)
        wqkv_sum[...] += tn(combined_grad, normed)
        branch = normalize_back(scaled, inverse, nt(combined_grad, wqkv_t_ref[...]))
        for i, s in enumerate(spots):
            for c in range(lanes):
                stream_rows[c, s, :] = branch[
                    i * all_frames : (i + 1) * all_frames, c * PAIR : (c + 1) * PAIR
                ]
        return carry

    for half in range(halves):

        def arrive(k):
            cot_copy(half, k).wait_recv()
            stream_copy(half, k).wait_recv()

        each_other(n, arrive)
        for c in range(lanes):
            part = slice(c * PAIR, (c + 1) * PAIR)
            flat = stream_rows.shape[1:]
            stream_rows[c] = stream_recv[half, :, :, part].astype(F32).reshape(flat)
            cot_rows[c] = cot_recv[half, :, :, part].astype(F32).reshape(flat)
        lax.fori_loop(0, span // few, temporal, 0)
        for c in range(lanes):
            part = stream_rows[c].reshape(branch_send.shape[1:3] + (PAIR,)).astype(BF16)
            branch_send[half, :, :, c * PAIR : (c + 1) * PAIR] = part
        for step in range(steps):
            each_other(n, lambda k: slab_copy(half, step, k).start())
        branch_recv[half, me] = branch_send[half, me]

    close(0)

    late = frames - together
    early = min(together, bits)

    def backward(step, carry):
        def arrive(k):
            for half in range(halves):
                slab_copy(half, step, k).wait_recv()

        each_other(n, arrive)
        for i, branch in enumerate(get(branch_recv, step)):
            frame = step * together + i
            for level in range(early if inside else 0):
                pl.when(frame == late + level)(functools.partial(advance, 0, level))
            stream_grad = (cot_ref[frame].astype(F32) + branch).astype(BF16)
            wo_sum[...] += tn(stream_grad, attended_s[frame])
            upstream = nt(stream_grad, wo_s_ref[...]).astype(BF16)
            combined = combined_s[frame]
            grads = []
            for pair in range(lanes):
                q, k, v = three(combined, pair, width)
                up = upstream[:, pair * PAIR : (pair + 1) * PAIR]
                grads.append(pair_backward(q, k, v, up, probs_s[frame, pair]))
            combined_grad = jnp.concatenate([g[j] for j in range(3) for g in grads], 1)
            scaled, inverse = normalize(x_ref[frame].astype(F32))
            wqkv_sum[...] += tn(combined_grad, scaled.astype(BF16))
            input_grad = nt(combined_grad, wqkv_s_ref[...])
            token_grad_ref[frame] = (
                stream_grad.astype(F32) + normalize_back(scaled, inverse, input_grad)
            ).astype(BF16)
        return carry

    lax.fori_loop(0, steps, backward, 0)
    close(1)
    if inside:
        for level in range(bits):
            advance(1, level)
            if early + level < bits:
                advance(0, early + level)

    def left(k):
        for half in range(halves):
            cot_copy(half, k).wait_send()
            stream_copy(half, k).wait_send()
            for step in range(steps):
                slab_copy(half, step, k).wait_send()

    each_other(n, left)


def scatter_sum(wqkv_grad, wo_grad, n):
    width = wqkv_grad.shape[1]
    mine = jnp.concatenate(
        [wqkv_grad.reshape(n, -1, width), wo_grad.reshape(n, -1, width)], 1
    )
    me = lax.axis_index("seq")
    bit = 1
    while bit < n:
        side = lax.rem(me // bit, 2)
        halves = mine.reshape((mine.shape[0] // 2, 2) + mine.shape[1:])
        keep = lax.dynamic_index_in_dim(halves, side, 1, keepdims=False)
        give = lax.dynamic_index_in_dim(halves, 1 - side, 1, keepdims=False).astype(BF16)
        pairs = [(i, i ^ bit) for i in range(n)]
        got = lax.ppermute(give, "seq", pairs)
        mine = keep.astype(F32) + got.astype(F32)
        bit *= 2
    mine = lax.psum(mine[0], "dp")
    split = wqkv_grad.shape[0] // n
    return mine[:split].T, mine[split:].T


def on_device(tokens, cotangent, wqkv_spatial, wo_spatial, wqkv_temporal, wo_temporal):
    clips, frames, count, width = tokens.shape
    n = lax.axis_size("seq")
    patches = count // n
    total = frames * clips
    pairs = width // PAIR
    halves = 2 if patches == 16 and total % 2 == 0 else 1
    span = patches // halves
    bits = n.bit_length() - 1
    split = width // n
    inside = n == 1 << bits and 4 * split % 16 == 0 and bits > 0
    owners = [int(format(i, "b").zfill(bits)[::-1], 2) for i in range(n if inside else 0)]
    places = np.zeros((8, 1), np.int32)
    if inside:
        own = [
            [3 * split * j + i for i in range(3 * split)]
            + [3 * width + split * j + i for i in range(split)]
            for j in owners
        ]
        places = np.array(own, np.int32).reshape(-1, 1)
    whole = pl.BlockSpec(memory_space=pltpu.VMEM)
    shape = jax.ShapeDtypeStruct
    sems = pltpu.SemaphoreType.DMA
    exchanged = pltpu.VMEM((halves, n, total * span, width), BF16)
    gathered = pltpu.VMEM((pairs, n * total * span, PAIR), F32)
    sums = shape((2, 4 * split, width), F32) if inside else shape((2, 4 * width, width), BF16)
    token_grad, grads = pl.pallas_call(
        functools.partial(kernel, n, halves, inside),
        in_specs=[whole] * 7,
        out_specs=[whole] * 2,
        out_shape=[shape((total, count, width), BF16), sums],
        scratch_shapes=[
            pltpu.VMEM((total, pairs, count, 2 * count), BF16),
            pltpu.VMEM((total, count, 3 * width), BF16),
            pltpu.VMEM((total, count, width), BF16),
        ]
        + [exchanged] * 6
        + [gathered] * 2
        + [
            pltpu.VMEM((3 * width, width), F32),
            pltpu.VMEM((width, width), F32),
            sems((2, halves, n)), sems((2, halves, n)),
            sems((2, halves, max(total // 2, 1), n)),
            pltpu.VMEM((2, 2 * width if inside else 8, width), F32),
            pltpu.VMEM((4 * width if inside else 16, width), BF16),
            pltpu.VMEM((2, 4 * width if inside else 16, width), BF16),
            pltpu.VMEM((2, 4 * width if inside else 16, width), BF16),
            sems((2, 2, max(bits, 1))),
        ],
        compiler_params=pltpu.CompilerParams(
            collective_id=0, has_side_effects=True, vmem_limit_bytes=VMEM_LIMIT
        ),
        name="space_time_backward",
    )(
        tokens.reshape(total, count, width), cotangent.reshape(total, count, width),
        wqkv_spatial, wo_spatial, wqkv_temporal, wo_temporal, jnp.asarray(places),
    )
    if inside:
        grads = lax.psum(grads, "dp")
        wqkv_t, wqkv_s = [part[: 3 * split].T for part in grads]
        wo_t, wo_s = [part[3 * split :].T for part in grads]
    else:
        wqkv_t, wo_t = scatter_sum(grads[0, : 3 * width], grads[0, 3 * width :], n)
        wqkv_s, wo_s = scatter_sum(grads[1, : 3 * width], grads[1, 3 * width :], n)
    return (token_grad.reshape(tokens.shape), wqkv_s, wo_s, wqkv_t, wo_t)


def solution(mesh):
    in_specs = (P("dp", "seq", None, None), P("dp", "seq", None, None), P(), P(), P(), P())
    out_specs = (
        P("dp", "seq", None, None),
        P(None, "seq"),
        P(None, "seq"),
        P(None, "seq"),
        P(None, "seq"),
    )
    return jax.shard_map(
        on_device, mesh=mesh, in_specs=in_specs, out_specs=out_specs, check_vma=False
    )
```
